32 devices in a mesh: gx: 4 (over z), gy: 2 (over y), gz: 4 (over x, core).
Axes of the slice: x: 2, y: 2, z: 4, core: 2. Of those that a mesh axis runs over, the one named last changes fastest.
Arguments:
- e_field: float32 [3, 32, 128, 256], P(None, 'gx', 'gz', 'gy'), may hold values from -6 to 6
- h_field: float32 [3, 32, 128, 256], P(None, 'gx', 'gz', 'gy'), may hold values from -6 to 6
- e_forward: float32 [3, 32, 128, 256], P(None, 'gx', 'gz', 'gy'), may hold values from -6 to 6
- e_coeff: float32 [32, 128, 256], P('gx', 'gz', 'gy'), may hold values from 0.1 to 0.5
- h_coeff: float32 [32, 128, 256], P('gx', 'gz', 'gy'), may hold values from 0.1 to 0.5
- dft_acc: float32 [16, 32, 128, 256], P(None, 'gx', 'gz', 'gy'), may hold values from -6 to 6
- design_mask: int32 [4, 4, 32], P('gx', 'gz', 'gy'), may hold values 0 or 1
- omega_t: float32 [8], replicated, may hold values from -3.140625 to 3.140625
- port_index: int32 [4], replicated, may hold values from 0 to 31
- port_owner: int32 [4], replicated, may hold values from 0 to 31
- port_modes: float32 [4, 2, 128, 256], P(None, None, 'gz', 'gy'), may hold values from -0.0234375 to 0.0234375
- monitor_acc: float32 [32, 16], P(('gx', 'gy', 'gz')), may hold values from -6 to 6
Outputs:
- e_next: float32 [3, 32, 128, 256], P(None, 'gx', 'gz', 'gy')
- h_next: float32 [3, 32, 128, 256], P(None, 'gx', 'gz', 'gy')
- dft_next: float32 [16, 32, 128, 256], P(None, 'gx', 'gz', 'gy')
- monitor_next: float32 [32, 16], P(('gx', 'gy', 'gz'))
The draws below stay inside these ranges and needn't reach their ends.
All inputs are finite; a program needn't handle non-finite values. No bound on the sum of `design_mask` on one device may be relied on, other than what follows from the above.
Results may differ from the reference program's by a relative error of at most 0.00011.
Values sent between devices are 32-bit elements; how exact they have to be, the bound alone decides.
A program may use at most 64 MiB of HBM per device.

```python
import math
import jax
import jax.numpy as jnp
from jax import lax

BX = 8
BY = 8
BZ = 32
NF = 8
NP = 4
NX = 32
NY = 256
NZ = 128
N_GX = 4
N_GY = 2
N_GZ = 4


def plant(array, key, low, top_value):
    extent = array.shape
    spot = [jax.random.randint(jax.random.fold_in(key, axis), (), 0, extent[axis]) for axis in range(len(extent))]
    array = array.at[tuple(spot)].set(low)
    longest = extent.index(max(extent))
    spot[longest] = (spot[longest] + 1) % extent[longest]
    return array.at[tuple(spot)].set(top_value)


def levels(key, shape, shards, least, high):
    def one(axis_at, shards_of):
        heights = jax.random.uniform(jax.random.fold_in(jax.random.fold_in(key, 6), axis_at), (shards_of,), jnp.float32, least / len(shards), high / len(shards))
        return jnp.repeat(jnp.exp(heights), shape[axis_at] // shards_of).reshape((-1,) + (1,) * (len(shape) - axis_at - 1))

    gain = one(*shards[0])
    for cut in shards[1:]:
        gain = gain * one(*cut)
    return gain


def normal_values(own_key, extent, width, limit, pieces=(), kind=jnp.bfloat16):
    array = width * jax.random.normal(own_key, extent, jnp.float32)
    if pieces:
        array = array * levels(own_key, extent, pieces, -0.22, 0.18)
    return jnp.clip(array, -limit, limit).astype(kind)


def setup_inputs(seed: int = 0) -> dict:
    key_of = jax.random.split(jax.random.key(seed), 13)
    return {
        "e_field": normal_values(key_of[0], (3, NX, NZ, NY), 1.0, 6.0, ((1, 4), (2, 4), (3, 2)), jnp.float32),
        "h_field": normal_values(key_of[1], (3, NX, NZ, NY), 1.0, 6.0, ((1, 4), (2, 4), (3, 2)), jnp.float32),
        "e_forward": normal_values(key_of[2], (3, NX, NZ, NY), 1.0, 6.0, ((1, 4), (2, 4), (3, 2)), jnp.float32),
        "e_coeff": jnp.clip(jnp.exp(math.log(0.5) - 1.609438 * jax.random.uniform(key_of[3], (NX, NZ, NY), jnp.float32) ** levels(key_of[3], (NX, NZ, NY), ((0, 4), (1, 4), (2, 2)), -0.2, 0.2)), 0.1, 0.5),
        "h_coeff": jnp.clip(jnp.exp(math.log(0.5) - 1.609438 * jax.random.uniform(key_of[4], (NX, NZ, NY), jnp.float32) ** levels(key_of[4], (NX, NZ, NY), ((0, 4), (1, 4), (2, 2)), -0.2, 0.2)), 0.1, 0.5),
        "dft_acc": normal_values(key_of[5], (2 * NF, NX, NZ, NY), 1.0, 6.0, ((1, 4), (2, 4), (3, 2)), jnp.float32),
        "design_mask": plant((jax.random.randint(key_of[6], (NX // BX, NZ // BZ, NY // BY), 0, 2) < 1).astype(jnp.int32), jax.random.fold_in(key_of[6], 1), 0, 1),
        "omega_t": jnp.clip(jax.random.uniform(key_of[7], (NF,), jnp.float32, -3.140625, 3.140625), -3.140625, 3.140625),
        "port_index": plant(jax.random.randint(key_of[8], (NP,), 0, NX), jax.random.fold_in(key_of[8], 1), 0, NX - 1).astype(jnp.int32),
        "port_owner": plant(jax.random.randint(key_of[9], (NP,), 0, N_GX * N_GY * N_GZ), jax.random.fold_in(key_of[9], 1), 0, (N_GX * N_GY * N_GZ) - 1).astype(jnp.int32),
        "port_modes": normal_values(key_of[10], (NP, 2, NZ, NY), (2 * NY * NZ) ** -0.5, 0.0234375, ((2, 4), (3, 2)), jnp.float32),
        "monitor_acc": normal_values(key_of[11], (N_GX * N_GY * N_GZ, 2 * NF), 1.0, 6.0, ((0, 32),), jnp.float32),
    }


def lower_diff(field, along):
    size = field.shape[along]
    before = jnp.concatenate([jnp.zeros_like(lax.slice_in_dim(field, 0, 1, axis=along)), lax.slice_in_dim(field, 0, size - 1, axis=along)], along)
    return field - before


def upper_diff(field, along):
    size = field.shape[along]
    after = jnp.concatenate([lax.slice_in_dim(field, 1, size, axis=along), jnp.zeros_like(lax.slice_in_dim(field, 0, 1, axis=along))], along)
    return after - field


def reference(e_field, h_field, e_forward, e_coeff, h_coeff, dft_acc, design_mask, omega_t, port_index, port_owner, port_modes, monitor_acc):
    curl_h = jnp.stack([
        lower_diff(h_field[2], 2) - lower_diff(h_field[1], 1),
        lower_diff(h_field[0], 1) - lower_diff(h_field[2], 0),
        lower_diff(h_field[1], 0) - lower_diff(h_field[0], 2)])
    e_next = e_field - e_coeff[None] * curl_h
    curl_e = jnp.stack([
        upper_diff(e_next[2], 2) - upper_diff(e_next[1], 1),
        upper_diff(e_next[0], 1) - upper_diff(e_next[2], 0),
        upper_diff(e_next[1], 0) - upper_diff(e_next[0], 2)])
    h_next = h_field + h_coeff[None] * curl_e
    weight = jnp.repeat(jnp.repeat(jnp.repeat(design_mask.astype(jnp.float32), BX, 0), BZ, 1), BY, 2)
    product = weight * jnp.sum(e_forward * e_next, axis=0)
    cosines = jnp.cos(omega_t)
    sines = jnp.sin(omega_t)
    phase = jnp.concatenate([cosines, -sines])
    dft_next = dft_acc + phase[:, None, None, None] * product[None]
    planes_y = e_next[1][port_index]
    planes_z = e_next[2][port_index]
    intersection = jnp.sum(port_modes[:, 0] * planes_y + port_modes[:, 1] * planes_z, axis=(1, 2))
    devices = monitor_acc.shape[0]
    owned = (port_owner[None, :] == jnp.arange(devices, dtype=jnp.int32)[:, None]).astype(jnp.float32)
    monitor_next = monitor_acc + jnp.dot(owned, intersection[:, None] * phase[None, :], precision=lax.Precision.HIGHEST)
    return e_next, h_next, dft_next, monitor_next
```

```python
import functools

import jax
import jax.numpy as jnp
from jax import lax
from jax.experimental import pallas as pl
from jax.experimental.pallas import tpu as pltpu
from jax.sharding import PartitionSpec as P

BY = 8
NF = 8
NP = 4
UNROLL = 32


def tiles(plane):
    return [plane[8 * q : 8 * q + 8] for q in range(plane.shape[0] // 8)]


def pack_lane(fields, lane_of, lane):
    packed = jnp.zeros((8, 128), jnp.float32)
    k = 0
    for plane in fields:
        for tile in tiles(plane):
            moved = pltpu.roll(tile, (k - lane_of) % 128, 1)
            packed = jnp.where(lane == k, moved, packed)
            k += 1
    return packed


def unpack_lane(packed, first, count, lane_of, keep):
    out = [pltpu.roll(packed, (lane_of - first - q) % 128, 1) for q in range(count)]
    return jnp.where(keep, jnp.concatenate(out, 0), 0.0)


def step(
    sizes, e_hbm, h_hbm, ef_hbm, ec_hbm, hc_hbm, dft_hbm, modes_hbm,
    mask_ref, omega_ref, pidx_ref, powner_ref, mon_ref,
    en, hn, dn, mon_out,
    ef, ec, hc, modes,
    hx_in, hy_in, hz_in, ex_in, ey_in, ez_in, hy_out, ey_out, mine, rows,
    load_sems, h_send, h_recv, e_send, e_recv, all_send, all_recv,
):
    n_gx, n_gy, n_gz = sizes
    n = n_gx * n_gy * n_gz
    a, b, c = lax.axis_index("gx"), lax.axis_index("gy"), lax.axis_index("gz")
    stride_x, stride_y = n_gy * n_gz, n_gz
    me = a * stride_x + b * stride_y + c
    nx, nz, ny = ec.shape
    zt = nz // 8

    def each_other(run):
        if n <= UNROLL:
            for k in range(1, n):
                run(k, lax.rem(me + k, n))
        else:
            lax.fori_loop(1, n, lambda k, _: (run(k, lax.rem(me + k, n)), 0)[1], 0)

    barrier = pltpu.get_barrier_semaphore()
    loads = [
        pltpu.make_async_copy(src, dst, load_sems.at[i])
        for i, (src, dst) in enumerate(
            [(h_hbm, hn), (e_hbm, en), (ec_hbm, ec), (modes_hbm, modes), (hc_hbm, hc), (ef_hbm, ef), (dft_hbm, dn)]
        )
    ]
    for load in loads[:3]:
        load.start()
    each_other(
        lambda k, dev: pl.semaphore_signal(
            barrier, inc=1, device_id=dev, device_id_type=pl.DeviceIdType.LOGICAL
        )
    )
    for load in loads[3:]:
        load.start()

    def remote(src, dst, send, recv, dev):
        return pltpu.make_async_remote_copy(
            src_ref=src, dst_ref=dst, send_sem=send, recv_sem=recv,
            device_id=dev, device_id_type=pl.DeviceIdType.LOGICAL,
        )

    up = [(a < n_gx - 1, stride_x), (b < n_gy - 1, stride_y), (c < n_gz - 1, 1)]
    down = [(a > 0, stride_x), (b > 0, stride_y), (c > 0, 1)]
    h_copies = [
        remote(src, dst, h_send.at[i], h_recv.at[i], jnp.where(up[i][0], me + up[i][1], 0))
        for i, (src, dst) in enumerate(
            [(hn.at[1:3, nx - 1], hx_in), (hy_out, hy_in), (hn.at[0:2, :, nz - 1], hz_in)]
        )
    ]
    e_copies = [
        remote(src, dst, e_send.at[i], e_recv.at[i], jnp.where(down[i][0], me - down[i][1], 0))
        for i, (src, dst) in enumerate(
            [(en.at[1:3, 0], ex_in), (ey_out, ey_in), (en.at[0:2, :, 0], ez_in)]
        )
    ]

    row = lax.broadcasted_iota(jnp.int32, (nz, ny), 0)
    lane = lax.broadcasted_iota(jnp.int32, (nz, ny), 1)
    lane8 = lax.broadcasted_iota(jnp.int32, (8, 128), 1)

    loads[0].wait()
    hy_out[...] = pack_lane(
        [hn[comp, x] for comp in (0, 2) for x in range(nx)], ny - 1, lane8
    )
    pl.semaphore_wait(barrier, n - 1)
    for i in (0, 2, 1):
        pl.when(up[i][0])(h_copies[i].start)

    sub8 = lax.broadcasted_iota(jnp.int32, (8, 128), 0)
    angle_rows = jnp.zeros((8, 128), jnp.float32)
    angle_lanes = jnp.zeros((8, 128), jnp.float32)
    for f in range(NF):
        angle_rows = jnp.where(sub8 == f, omega_ref[f], angle_rows)
        angle_lanes = jnp.where((lane8 == f) | (lane8 == f + NF), omega_ref[f], angle_lanes)
    cosines, sines = jnp.cos(angle_rows), -jnp.sin(angle_rows)
    phase_lanes = jnp.where(lane8 < NF, jnp.cos(angle_lanes), -jnp.sin(angle_lanes))
    weight = jnp.zeros((8, 128), jnp.float32)
    for k in range(ny // BY):
        weight = jnp.where(lane8 // BY == k, mask_ref[0, 0, k].astype(jnp.float32), weight)
    weight = jnp.concatenate([weight] * zt, 0)

    loads[1].wait()
    loads[2].wait()

    def low(plane, axis):
        first = (row if axis == 0 else lane) == 0
        return plane - jnp.where(first, 0.0, pltpu.roll(plane, 1, axis))

    for x in range(nx):
        h0, h1, h2 = hn[0, x], hn[1, x], hn[2, x]
        d1 = h1 - hn[1, x - 1] if x else h1
        d2 = h2 - hn[2, x - 1] if x else h2
        coef = ec[x]
        en[0, x] = en[0, x] - coef * (low(h2, 1) - low(h1, 0))
        en[1, x] = en[1, x] - coef * (low(h0, 0) - d2)
        en[2, x] = en[2, x] - coef * (d1 - low(h0, 1))

    for i, landing in enumerate((hx_in, hy_in, hz_in)):
        pl.when(down[i][0])(h_copies[i].wait_recv)

        @pl.when(jnp.logical_not(down[i][0]))
        def _(landing=landing):
            landing[...] = jnp.zeros_like(landing)

    packed = hy_in[...]
    for x in range(nx):
        coef = ec[x]
        y0 = unpack_lane(packed, x * zt, zt, 0, lane == 0)
        y2 = unpack_lane(packed, (nx + x) * zt, zt, 0, lane == 0)
        z0 = jnp.where(sub8 == 0, hz_in[0, x : x + 1, :], 0.0)
        z1 = jnp.where(sub8 == 0, hz_in[1, x : x + 1, :], 0.0)
        rest = jnp.zeros((nz - 8, ny), jnp.float32)
        z0, z1 = jnp.concatenate([z0, rest], 0), jnp.concatenate([z1, rest], 0)
        add0, add1, add2 = y2 - z1, z0, -y0
        if x == 0:
            add1 = add1 - hx_in[1]
            add2 = add2 + hx_in[0]
        en[0, x] = en[0, x] + coef * add0
        en[1, x] = en[1, x] + coef * add1
        en[2, x] = en[2, x] + coef * add2

    loads[3].wait()
    share = jnp.zeros((8, 128), jnp.float32)
    for p in range(NP):
        x_of = pidx_ref[p] - a * nx
        inside = (x_of >= 0) & (x_of < nx)
        at = jnp.clip(x_of, 0, nx - 1)
        both = modes[p, 0] * en[1, at] + modes[p, 1] * en[2, at]
        total = functools.reduce(jnp.add, tiles(both))
        total = jnp.sum(jnp.sum(total, axis=0, keepdims=True), axis=1, keepdims=True)
        total = jnp.where(inside, total, 0.0)
        share = jnp.where(lane8 == p, total, share)
    mine[...] = share[0:1]

    def send_row(k, dev):
        remote(mine, rows.at[k - 1], all_send, all_recv, dev).start()

    each_other(send_row)
    for i in (0, 2):
        pl.when(down[i][0])(e_copies[i].start)
    ey_out[...] = pack_lane([en[comp, x] for comp in (0, 2) for x in range(nx)], 0, lane8)
    pl.when(down[1][0])(e_copies[1].start)

    for i in range(3):
        pl.when(up[i][0])(h_copies[i].wait_send)
    loads[4].wait()

    def high(plane, axis):
        last = (row == nz - 1) if axis == 0 else (lane == ny - 1)
        return jnp.where(last, 0.0, pltpu.roll(plane, plane.shape[axis] - 1, axis)) - plane

    for x in range(nx):
        e0, e1, e2 = en[0, x], en[1, x], en[2, x]
        d1 = en[1, x + 1] - e1 if x < nx - 1 else -e1
        d2 = en[2, x + 1] - e2 if x < nx - 1 else -e2
        coef = hc[x]
        hn[0, x] = hn[0, x] + coef * (high(e2, 1) - high(e1, 0))
        hn[1, x] = hn[1, x] + coef * (high(e0, 0) - d2)
        hn[2, x] = hn[2, x] + coef * (d1 - high(e0, 1))

    loads[5].wait()
    loads[6].wait()
    for x in range(nx):
        product = weight * (ef[0, x] * en[0, x] + ef[1, x] * en[1, x] + ef[2, x] * en[2, x])
        for f in range(NF):
            dn[f, x] = dn[f, x] + cosines[f : f + 1] * product
            dn[NF + f, x] = dn[NF + f, x] + sines[f : f + 1] * product

    for i, landing in enumerate((ex_in, ey_in, ez_in)):
        pl.when(up[i][0])(e_copies[i].wait_recv)

        @pl.when(jnp.logical_not(up[i][0]))
        def _(landing=landing):
            landing[...] = jnp.zeros_like(landing)

    packed = ey_in[...]
    for x in range(nx):
        coef = hc[x]
        y0 = unpack_lane(packed, x * zt, zt, ny - 1, lane == ny - 1)
        y2 = unpack_lane(packed, (nx + x) * zt, zt, ny - 1, lane == ny - 1)
        z0 = jnp.where(sub8 == 7, ez_in[0, x : x + 1, :], 0.0)
        z1 = jnp.where(sub8 == 7, ez_in[1, x : x + 1, :], 0.0)
        rest = jnp.zeros((nz - 8, ny), jnp.float32)
        z0, z1 = jnp.concatenate([rest, z0], 0), jnp.concatenate([rest, z1], 0)
        add0, add1, add2 = y2 - z1, z0, -y0
        if x == nx - 1:
            add1 = add1 - ex_in[1]
            add2 = add2 + ex_in[0]
        hn[0, x] = hn[0, x] + coef * add0
        hn[1, x] = hn[1, x] + coef * add1
        hn[2, x] = hn[2, x] + coef * add2
    for i in range(3):
        pl.when(down[i][0])(e_copies[i].wait_send)

    remote(rows, rows, all_send, all_recv, me).wait()
    intersection = jnp.sum(rows[...], axis=0) + mine[...]
    lane1 = lax.broadcasted_iota(jnp.int32, (1, 128), 1)
    owned = jnp.zeros((1, 128), jnp.float32)
    for p in range(NP):
        owned = jnp.where(lane1 == p, (powner_ref[p] == me).astype(jnp.float32), owned)
    total = jnp.sum(owned * intersection, axis=1, keepdims=True)
    mon_out[...] = mon_ref[...] + total * phase_lanes[0:1, : 2 * NF]


def write_out(en, hn, dn, mon, en_out, hn_out, dn_out, mon_out, sems):
    parts = 4
    size = dn.shape[0] // parts
    pairs = [(dn.at[pl.ds(i * size, size)], dn_out.at[pl.ds(i * size, size)]) for i in range(parts)]
    pairs += [(en, en_out), (hn, hn_out), (mon, mon_out)]
    copies = [pltpu.make_async_copy(src, dst, sems.at[i]) for i, (src, dst) in enumerate(pairs)]
    for copy in copies:
        copy.start()
    for copy in copies:
        copy.wait()


def body(sizes, e_field, h_field, e_forward, e_coeff, h_coeff, dft_acc, design_mask,
         omega_t, port_index, port_owner, port_modes, monitor_acc):
    n = sizes[0] * sizes[1] * sizes[2]
    nx, nz, ny = e_coeff.shape
    f32 = jnp.float32
    hbm = pl.BlockSpec(memory_space=pltpu.HBM)
    vmem = pl.BlockSpec(memory_space=pltpu.VMEM)
    smem = pl.BlockSpec(memory_space=pltpu.SMEM)
    held = pl.pallas_call(
        functools.partial(step, sizes),
        out_shape=[
            pltpu.VMEM(e_field.shape, f32),
            pltpu.VMEM(h_field.shape, f32),
            pltpu.VMEM(dft_acc.shape, f32),
            pltpu.VMEM(monitor_acc.shape, f32),
        ],
        in_specs=[hbm] * 7 + [smem] * 4 + [vmem],
        out_specs=[vmem] * 4,
        scratch_shapes=[
            pltpu.VMEM(e_forward.shape, f32),
            pltpu.VMEM(e_coeff.shape, f32),
            pltpu.VMEM(h_coeff.shape, f32),
            pltpu.VMEM(port_modes.shape, f32),
            pltpu.VMEM((2, nz, ny), f32),
            pltpu.VMEM((8, 128), f32),
            pltpu.VMEM((2, nx, ny), f32),
            pltpu.VMEM((2, nz, ny), f32),
            pltpu.VMEM((8, 128), f32),
            pltpu.VMEM((2, nx, ny), f32),
            pltpu.VMEM((8, 128), f32),
            pltpu.VMEM((8, 128), f32),
            pltpu.VMEM((1, 128), f32),
            pltpu.VMEM((n - 1, 1, 128), f32),
            pltpu.SemaphoreType.DMA((7,)),
            pltpu.SemaphoreType.DMA((3,)),
            pltpu.SemaphoreType.DMA((3,)),
            pltpu.SemaphoreType.DMA((3,)),
            pltpu.SemaphoreType.DMA((3,)),
            pltpu.SemaphoreType.DMA,
            pltpu.SemaphoreType.DMA,
        ],
        compiler_params=pltpu.CompilerParams(
            collective_id=0, has_side_effects=True, vmem_limit_bytes=24 * 2**20
        ),
        name="yee_step",
    )(e_field, h_field, e_forward, e_coeff, h_coeff, dft_acc, port_modes,
      design_mask, omega_t, port_index, port_owner, monitor_acc)
    shape = lambda x: jax.ShapeDtypeStruct(x.shape, f32)
    return pl.pallas_call(
        write_out,
        out_shape=[shape(x) for x in (e_field, h_field, dft_acc, monitor_acc)],
        in_specs=[vmem] * 4,
        out_specs=[hbm] * 4,
        scratch_shapes=[pltpu.SemaphoreType.DMA((7,))],
        name="write_out",
    )(*held)


def solution(mesh):
    grid = P(None, "gx", "gz", "gy")
    brick = P("gx", "gz", "gy")
    own = P(("gx", "gy", "gz"), None)
    sizes = tuple(mesh.shape[axis] for axis in ("gx", "gy", "gz"))
    in_specs = (grid, grid, grid, brick, brick, grid, brick, P(), P(), P(),
                P(None, None, "gz", "gy"), own)
    return jax.shard_map(
        functools.partial(body, sizes), mesh=mesh, in_specs=in_specs,
        out_specs=(grid, grid, grid, own), check_vma=False,
    )
```

```python
import functools

import jax
import jax.numpy as jnp
from jax import lax
from jax.experimental import pallas as pl
from jax.experimental.pallas import tpu as pltpu
from jax.sharding import PartitionSpec as P

BY = 8
NF = 8
NP = 4
UNROLL = 32


def tiles(plane):
    return [plane[8 * q : 8 * q + 8] for q in range(plane.shape[0] // 8)]


def pack_lane(fields, lane_of, lane):
    packed = jnp.zeros((8, 128), jnp.float32)
    k = 0
    for plane in fields:
        for tile in tiles(plane):
            moved = pltpu.roll(tile, (k - lane_of) % 128, 1)
            packed = jnp.where(lane == k, moved, packed)
            k += 1
    return packed


def unpack_lane(packed, first, count, lane_of, keep):
    out = [pltpu.roll(packed, (lane_of - first - q) % 128, 1) for q in range(count)]
    return jnp.where(keep, jnp.concatenate(out, 0), 0.0)


def step(
    sizes, e_hbm, h_hbm, ef_hbm, ec_hbm, hc_hbm, dft_hbm, modes_hbm,
    mask_hbm, omega_hbm, pidx_hbm, powner_hbm, mon_hbm,
    en, hn, dn, mon_out,
    ef, ec, hc, modes, mask_ref, omega_ref, pidx_ref, powner_ref, mon_ref,
    hx_in, hy_in, hz_in, ex_in, ey_in, ez_in, hy_out, ey_out, mine, rows,
    load_sems, h_send, h_recv, e_send, e_recv, all_send, all_recv,
):
    n_gx, n_gy, n_gz = sizes
    n = n_gx * n_gy * n_gz
    a, b, c = lax.axis_index("gx"), lax.axis_index("gy"), lax.axis_index("gz")
    stride_x, stride_y = n_gy * n_gz, n_gz
    me = a * stride_x + b * stride_y + c
    nx, nz, ny = ec.shape
    zt = nz // 8

    def each_other(run):
        if n <= UNROLL:
            for k in range(1, n):
                run(k, lax.rem(me + k, n))
        else:
            lax.fori_loop(1, n, lambda k, _: (run(k, lax.rem(me + k, n)), 0)[1], 0)

    barrier = pltpu.get_barrier_semaphore()
    loads = [
        pltpu.make_async_copy(src, dst, load_sems.at[i])
        for i, (src, dst) in enumerate(
            [(h_hbm, hn), (e_hbm, en), (ec_hbm, ec), (modes_hbm, modes), (hc_hbm, hc), (ef_hbm, ef), (dft_hbm, dn),
             (mask_hbm, mask_ref), (omega_hbm, omega_ref), (pidx_hbm, pidx_ref), (powner_hbm, powner_ref), (mon_hbm, mon_ref)]
        )
    ]
    for load in loads[:3]:
        load.start()
    each_other(
        lambda k, dev: pl.semaphore_signal(
            barrier, inc=1, device_id=dev, device_id_type=pl.DeviceIdType.LOGICAL
        )
    )
    for load in loads[7:] + loads[3:7]:
        load.start()

    def remote(src, dst, send, recv, dev):
        return pltpu.make_async_remote_copy(
            src_ref=src, dst_ref=dst, send_sem=send, recv_sem=recv,
            device_id=dev, device_id_type=pl.DeviceIdType.LOGICAL,
        )

    up = [(a < n_gx - 1, stride_x), (b < n_gy - 1, stride_y), (c < n_gz - 1, 1)]
    down = [(a > 0, stride_x), (b > 0, stride_y), (c > 0, 1)]
    h_copies = [
        remote(src, dst, h_send.at[i], h_recv.at[i], jnp.where(up[i][0], me + up[i][1], 0))
        for i, (src, dst) in enumerate(
            [(hn.at[1:3, nx - 1], hx_in), (hy_out, hy_in), (hn.at[0:2, :, nz - 1], hz_in)]
        )
    ]
    e_copies = [
        remote(src, dst, e_send.at[i], e_recv.at[i], jnp.where(down[i][0], me - down[i][1], 0))
        for i, (src, dst) in enumerate(
            [(en.at[1:3, 0], ex_in), (ey_out, ey_in), (en.at[0:2, :, 0], ez_in)]
        )
    ]

    row = lax.broadcasted_iota(jnp.int32, (nz, ny), 0)
    lane = lax.broadcasted_iota(jnp.int32, (nz, ny), 1)
    lane8 = lax.broadcasted_iota(jnp.int32, (8, 128), 1)

    loads[0].wait()
    hy_out[...] = pack_lane(
        [hn[comp, x] for comp in (0, 2) for x in range(nx)], ny - 1, lane8
    )
    pl.semaphore_wait(barrier, n - 1)
    for i in (0, 2, 1):
        pl.when(up[i][0])(h_copies[i].start)

    for load in loads[7:]:
        load.wait()
    sub8 = lax.broadcasted_iota(jnp.int32, (8, 128), 0)
    angle_rows = jnp.zeros((8, 128), jnp.float32)
    angle_lanes = jnp.zeros((8, 128), jnp.float32)
    for f in range(NF):
        angle_rows = jnp.where(sub8 == f, omega_ref[f], angle_rows)
        angle_lanes = jnp.where((lane8 == f) | (lane8 == f + NF), omega_ref[f], angle_lanes)
    cosines, sines = jnp.cos(angle_rows), -jnp.sin(angle_rows)
    phase_lanes = jnp.where(lane8 < NF, jnp.cos(angle_lanes), -jnp.sin(angle_lanes))
    weight = jnp.zeros((8, 128), jnp.float32)
    for k in range(ny // BY):
        weight = jnp.where(lane8 // BY == k, mask_ref[0, 0, k].astype(jnp.float32), weight)
    weight = jnp.concatenate([weight] * zt, 0)

    loads[1].wait()
    loads[2].wait()

    def low(plane, axis):
        first = (row if axis == 0 else lane) == 0
        return plane - jnp.where(first, 0.0, pltpu.roll(plane, 1, axis))

    for x in range(nx):
        h0, h1, h2 = hn[0, x], hn[1, x], hn[2, x]
        d1 = h1 - hn[1, x - 1] if x else h1
        d2 = h2 - hn[2, x - 1] if x else h2
        coef = ec[x]
        en[0, x] = en[0, x] - coef * (low(h2, 1) - low(h1, 0))
        en[1, x] = en[1, x] - coef * (low(h0, 0) - d2)
        en[2, x] = en[2, x] - coef * (d1 - low(h0, 1))

    for i, landing in enumerate((hx_in, hy_in, hz_in)):
        pl.when(down[i][0])(h_copies[i].wait_recv)

        @pl.when(jnp.logical_not(down[i][0]))
        def _(landing=landing):
            landing[...] = jnp.zeros_like(landing)

    packed = hy_in[...]
    for x in range(nx):
        coef = ec[x]
        y0 = unpack_lane(packed, x * zt, zt, 0, lane == 0)
        y2 = unpack_lane(packed, (nx + x) * zt, zt, 0, lane == 0)
        z0 = jnp.where(sub8 == 0, hz_in[0, x : x + 1, :], 0.0)
        z1 = jnp.where(sub8 == 0, hz_in[1, x : x + 1, :], 0.0)
        rest = jnp.zeros((nz - 8, ny), jnp.float32)
        z0, z1 = jnp.concatenate([z0, rest], 0), jnp.concatenate([z1, rest], 0)
        add0, add1, add2 = y2 - z1, z0, -y0
        if x == 0:
            add1 = add1 - hx_in[1]
            add2 = add2 + hx_in[0]
        en[0, x] = en[0, x] + coef * add0
        en[1, x] = en[1, x] + coef * add1
        en[2, x] = en[2, x] + coef * add2

    loads[3].wait()
    share = jnp.zeros((8, 128), jnp.float32)
    for p in range(NP):
        x_of = pidx_ref[p] - a * nx
        inside = (x_of >= 0) & (x_of < nx)
        at = jnp.clip(x_of, 0, nx - 1)
        both = modes[p, 0] * en[1, at] + modes[p, 1] * en[2, at]
        total = functools.reduce(jnp.add, tiles(both))
        total = jnp.sum(jnp.sum(total, axis=0, keepdims=True), axis=1, keepdims=True)
        total = jnp.where(inside, total, 0.0)
        share = jnp.where(lane8 == p, total, share)
    mine[...] = share[0:1]

    def send_row(k, dev):
        remote(mine, rows.at[k - 1], all_send, all_recv, dev).start()

    each_other(send_row)
    for i in (0, 2):
        pl.when(down[i][0])(e_copies[i].start)
    ey_out[...] = pack_lane([en[comp, x] for comp in (0, 2) for x in range(nx)], 0, lane8)
    pl.when(down[1][0])(e_copies[1].start)

    for i in range(3):
        pl.when(up[i][0])(h_copies[i].wait_send)
    loads[4].wait()

    def high(plane, axis):
        last = (row == nz - 1) if axis == 0 else (lane == ny - 1)
        return jnp.where(last, 0.0, pltpu.roll(plane, plane.shape[axis] - 1, axis)) - plane

    for x in range(nx):
        e0, e1, e2 = en[0, x], en[1, x], en[2, x]
        d1 = en[1, x + 1] - e1 if x < nx - 1 else -e1
        d2 = en[2, x + 1] - e2 if x < nx - 1 else -e2
        coef = hc[x]
        hn[0, x] = hn[0, x] + coef * (high(e2, 1) - high(e1, 0))
        hn[1, x] = hn[1, x] + coef * (high(e0, 0) - d2)
        hn[2, x] = hn[2, x] + coef * (d1 - high(e0, 1))

    loads[5].wait()
    loads[6].wait()
    for x in range(nx):
        product = weight * (ef[0, x] * en[0, x] + ef[1, x] * en[1, x] + ef[2, x] * en[2, x])
        for f in range(NF):
            dn[f, x] = dn[f, x] + cosines[f : f + 1] * product
            dn[NF + f, x] = dn[NF + f, x] + sines[f : f + 1] * product

    for i, landing in enumerate((ex_in, ey_in, ez_in)):
        pl.when(up[i][0])(e_copies[i].wait_recv)

        @pl.when(jnp.logical_not(up[i][0]))
        def _(landing=landing):
            landing[...] = jnp.zeros_like(landing)

    packed = ey_in[...]
    for x in range(nx):
        coef = hc[x]
        y0 = unpack_lane(packed, x * zt, zt, ny - 1, lane == ny - 1)
        y2 = unpack_lane(packed, (nx + x) * zt, zt, ny - 1, lane == ny - 1)
        z0 = jnp.where(sub8 == 7, ez_in[0, x : x + 1, :], 0.0)
        z1 = jnp.where(sub8 == 7, ez_in[1, x : x + 1, :], 0.0)
        rest = jnp.zeros((nz - 8, ny), jnp.float32)
        z0, z1 = jnp.concatenate([rest, z0], 0), jnp.concatenate([rest, z1], 0)
        add0, add1, add2 = y2 - z1, z0, -y0
        if x == nx - 1:
            add1 = add1 - ex_in[1]
            add2 = add2 + ex_in[0]
        hn[0, x] = hn[0, x] + coef * add0
        hn[1, x] = hn[1, x] + coef * add1
        hn[2, x] = hn[2, x] + coef * add2
    for i in range(3):
        pl.when(down[i][0])(e_copies[i].wait_send)

    remote(rows, rows, all_send, all_recv, me).wait()
    intersection = jnp.sum(rows[...], axis=0) + mine[...]
    lane1 = lax.broadcasted_iota(jnp.int32, (1, 128), 1)
    owned = jnp.zeros((1, 128), jnp.float32)
    for p in range(NP):
        owned = jnp.where(lane1 == p, (powner_ref[p] == me).astype(jnp.float32), owned)
    total = jnp.sum(owned * intersection, axis=1, keepdims=True)
    mon_out[...] = mon_ref[...] + total * phase_lanes[0:1, : 2 * NF]


def write_out(en, hn, dn, mon, en_out, hn_out, dn_out, mon_out, sems):
    parts = 4
    size = dn.shape[0] // parts
    pairs = [(dn.at[pl.ds(i * size, size)], dn_out.at[pl.ds(i * size, size)]) for i in range(parts)]
    pairs += [(en, en_out), (hn, hn_out), (mon, mon_out)]
    copies = [pltpu.make_async_copy(src, dst, sems.at[i]) for i, (src, dst) in enumerate(pairs)]
    for copy in copies:
        copy.start()
    for copy in copies:
        copy.wait()


def body(sizes, e_field, h_field, e_forward, e_coeff, h_coeff, dft_acc, design_mask,
         omega_t, port_index, port_owner, port_modes, monitor_acc):
    n = sizes[0] * sizes[1] * sizes[2]
    nx, nz, ny = e_coeff.shape
    f32 = jnp.float32
    hbm = pl.BlockSpec(memory_space=pltpu.HBM)
    vmem = pl.BlockSpec(memory_space=pltpu.VMEM)
    far = lambda x: pltpu.with_memory_space_constraint(x, pltpu.HBM)
    held = pl.pallas_call(
        functools.partial(step, sizes),
        out_shape=[
            pltpu.VMEM(e_field.shape, f32),
            pltpu.VMEM(h_field.shape, f32),
            pltpu.VMEM(dft_acc.shape, f32),
            pltpu.VMEM(monitor_acc.shape, f32),
        ],
        in_specs=[hbm] * 12,
        out_specs=[vmem] * 4,
        scratch_shapes=[
            pltpu.VMEM(e_forward.shape, f32),
            pltpu.VMEM(e_coeff.shape, f32),
            pltpu.VMEM(h_coeff.shape, f32),
            pltpu.VMEM(port_modes.shape, f32),
            pltpu.SMEM(design_mask.shape, jnp.int32),
            pltpu.SMEM(omega_t.shape, f32),
            pltpu.SMEM(port_index.shape, jnp.int32),
            pltpu.SMEM(port_owner.shape, jnp.int32),
            pltpu.VMEM(monitor_acc.shape, f32),
            pltpu.VMEM((2, nz, ny), f32),
            pltpu.VMEM((8, 128), f32),
            pltpu.VMEM((2, nx, ny), f32),
            pltpu.VMEM((2, nz, ny), f32),
            pltpu.VMEM((8, 128), f32),
            pltpu.VMEM((2, nx, ny), f32),
            pltpu.VMEM((8, 128), f32),
            pltpu.VMEM((8, 128), f32),
            pltpu.VMEM((1, 128), f32),
            pltpu.VMEM((n - 1, 1, 128), f32),
            pltpu.SemaphoreType.DMA((12,)),
            pltpu.SemaphoreType.DMA((3,)),
            pltpu.SemaphoreType.DMA((3,)),
            pltpu.SemaphoreType.DMA((3,)),
            pltpu.SemaphoreType.DMA((3,)),
            pltpu.SemaphoreType.DMA,
            pltpu.SemaphoreType.DMA,
        ],
        compiler_params=pltpu.CompilerParams(
            collective_id=0, has_side_effects=True, vmem_limit_bytes=24 * 2**20
        ),
        name="yee_step",
    )(*map(far, (e_field, h_field, e_forward, e_coeff, h_coeff, dft_acc, port_modes,
      design_mask, omega_t, port_index, port_owner, monitor_acc)))
    shape = lambda x: jax.ShapeDtypeStruct(x.shape, f32)
    return pl.pallas_call(
        write_out,
        out_shape=[shape(x) for x in (e_field, h_field, dft_acc, monitor_acc)],
        in_specs=[vmem] * 4,
        out_specs=[hbm] * 4,
        scratch_shapes=[pltpu.SemaphoreType.DMA((7,))],
        name="write_out",
    )(*[pltpu.with_memory_space_constraint(x, pltpu.VMEM) for x in held])


def solution(mesh):
    grid = P(None, "gx", "gz", "gy")
    brick = P("gx", "gz", "gy")
    own = P(("gx", "gy", "gz"), None)
    sizes = tuple(mesh.shape[axis] for axis in ("gx", "gy", "gz"))
    in_specs = (grid, grid, grid, brick, brick, grid, brick, P(), P(), P(),
                P(None, None, "gz", "gy"), own)
    return jax.shard_map(
        functools.partial(body, sizes), mesh=mesh, in_specs=in_specs,
        out_specs=(grid, grid, grid, own), check_vma=False,
    )
```

```python
import functools

import jax
import jax.numpy as jnp
from jax import lax
from jax.experimental import pallas as pl
from jax.experimental.pallas import tpu as pltpu
from jax.sharding import PartitionSpec as P

BY = 8
NF = 8
NP = 4
UNROLL = 32


def tiles(plane):
    return [plane[8 * q : 8 * q + 8] for q in range(plane.shape[0] // 8)]


def pack_lane(fields, lane_of, lane):
    packed = jnp.zeros((8, 128), jnp.float32)
    k = 0
    for plane in fields:
        for tile in tiles(plane):
            moved = pltpu.roll(tile, (k - lane_of) % 128, 1)
            packed = jnp.where(lane == k, moved, packed)
            k += 1
    return packed


def unpack_lane(packed, first, count, lane_of, keep):
    out = [pltpu.roll(packed, (lane_of - first - q) % 128, 1) for q in range(count)]
    return jnp.where(keep, jnp.concatenate(out, 0), 0.0)


def step(
    sizes, e_hbm, h_hbm, ef_hbm, ec_hbm, hc_hbm, dft_hbm, modes_hbm,
    mask_hbm, omega_hbm, pidx_hbm, powner_hbm, mon_hbm,
    en, hn, dn, mon_out,
    ef, ec, hc, modes, mask_ref, omega_ref, pidx_ref, powner_ref, mon_ref,
    hx_in, hy_in, hz_in, ex_in, ey_in, ez_in, hy_out, ey_out, mine, rows,
    load_sems, h_send, h_recv, e_send, e_recv, all_send, all_recv, known_sems,
):
    n_gx, n_gy, n_gz = sizes
    n = n_gx * n_gy * n_gz
    a, b, c = lax.axis_index("gx"), lax.axis_index("gy"), lax.axis_index("gz")
    stride_x, stride_y = n_gy * n_gz, n_gz
    me = a * stride_x + b * stride_y + c
    nx, nz, ny = ec.shape
    zt = nz // 8

    lines = [(a, n_gx, stride_x), (b, n_gy, stride_y), (c, n_gz, 1)]
    partners = [
        [me + (lax.rem(at + k, size) - at) * stride for k in range(1, size)]
        for at, size, stride in lines
    ]

    barrier = pltpu.get_barrier_semaphore()
    loads = [
        pltpu.make_async_copy(src, dst, load_sems.at[i])
        for i, (src, dst) in enumerate(
            [(h_hbm, hn), (e_hbm, en), (ec_hbm, ec), (modes_hbm, modes), (hc_hbm, hc), (ef_hbm, ef), (dft_hbm, dn),
             (mask_hbm, mask_ref), (omega_hbm, omega_ref), (pidx_hbm, pidx_ref), (powner_hbm, powner_ref), (mon_hbm, mon_ref)]
        )
    ]
    for load in loads[:3]:
        load.start()
    for line in partners:
        for dev in line:
            pl.semaphore_signal(
                barrier, inc=1, device_id=dev, device_id_type=pl.DeviceIdType.LOGICAL
            )
    for load in loads[7:] + loads[3:7]:
        load.start()

    def remote(src, dst, send, recv, dev):
        return pltpu.make_async_remote_copy(
            src_ref=src, dst_ref=dst, send_sem=send, recv_sem=recv,
            device_id=dev, device_id_type=pl.DeviceIdType.LOGICAL,
        )

    up = [(a < n_gx - 1, stride_x), (b < n_gy - 1, stride_y), (c < n_gz - 1, 1)]
    down = [(a > 0, stride_x), (b > 0, stride_y), (c > 0, 1)]
    h_copies = [
        remote(src, dst, h_send.at[i], h_recv.at[i], jnp.where(up[i][0], me + up[i][1], 0))
        for i, (src, dst) in enumerate(
            [(hn.at[1:3, nx - 1], hx_in), (hy_out, hy_in), (hn.at[0:2, :, nz - 1], hz_in)]
        )
    ]
    e_copies = [
        remote(src, dst, e_send.at[i], e_recv.at[i], jnp.where(down[i][0], me - down[i][1], 0))
        for i, (src, dst) in enumerate(
            [(en.at[1:3, 0], ex_in), (ey_out, ey_in), (en.at[0:2, :, 0], ez_in)]
        )
    ]

    row = lax.broadcasted_iota(jnp.int32, (nz, ny), 0)
    lane = lax.broadcasted_iota(jnp.int32, (nz, ny), 1)
    lane8 = lax.broadcasted_iota(jnp.int32, (8, 128), 1)

    loads[0].wait()
    hy_out[...] = pack_lane(
        [hn[comp, x] for comp in (0, 2) for x in range(nx)], ny - 1, lane8
    )
    pl.semaphore_wait(barrier, sum(map(len, partners)))
    for i in (0, 2, 1):
        pl.when(up[i][0])(h_copies[i].start)

    def tell(line, sem):
        for dev in line:
            pl.semaphore_signal(
                sem, inc=1, device_id=dev, device_id_type=pl.DeviceIdType.LOGICAL
            )

    tell(partners[1], known_sems.at[0])

    for load in loads[7:]:
        load.wait()
    sub8 = lax.broadcasted_iota(jnp.int32, (8, 128), 0)
    angle_rows = jnp.zeros((8, 128), jnp.float32)
    angle_lanes = jnp.zeros((8, 128), jnp.float32)
    for f in range(NF):
        angle_rows = jnp.where(sub8 == f, omega_ref[f], angle_rows)
        angle_lanes = jnp.where((lane8 == f) | (lane8 == f + NF), omega_ref[f], angle_lanes)
    cosines, sines = jnp.cos(angle_rows), -jnp.sin(angle_rows)
    phase_lanes = jnp.where(lane8 < NF, jnp.cos(angle_lanes), -jnp.sin(angle_lanes))
    weight = jnp.zeros((8, 128), jnp.float32)
    for k in range(ny // BY):
        weight = jnp.where(lane8 // BY == k, mask_ref[0, 0, k].astype(jnp.float32), weight)
    weight = jnp.concatenate([weight] * zt, 0)

    loads[1].wait()
    loads[2].wait()

    def low(plane, axis):
        first = (row if axis == 0 else lane) == 0
        return plane - jnp.where(first, 0.0, pltpu.roll(plane, 1, axis))

    for x in range(nx):
        h0, h1, h2 = hn[0, x], hn[1, x], hn[2, x]
        d1 = h1 - hn[1, x - 1] if x else h1
        d2 = h2 - hn[2, x - 1] if x else h2
        coef = ec[x]
        en[0, x] = en[0, x] - coef * (low(h2, 1) - low(h1, 0))
        en[1, x] = en[1, x] - coef * (low(h0, 0) - d2)
        en[2, x] = en[2, x] - coef * (d1 - low(h0, 1))

    if n_gy > 1:
        pl.semaphore_wait(known_sems.at[0], n_gy - 1)
    tell(partners[2], known_sems.at[1])

    for i, landing in enumerate((hx_in, hy_in, hz_in)):
        pl.when(down[i][0])(h_copies[i].wait_recv)

        @pl.when(jnp.logical_not(down[i][0]))
        def _(landing=landing):
            landing[...] = jnp.zeros_like(landing)

    packed = hy_in[...]
    for x in range(nx):
        coef = ec[x]
        y0 = unpack_lane(packed, x * zt, zt, 0, lane == 0)
        y2 = unpack_lane(packed, (nx + x) * zt, zt, 0, lane == 0)
        z0 = jnp.where(sub8 == 0, hz_in[0, x : x + 1, :], 0.0)
        z1 = jnp.where(sub8 == 0, hz_in[1, x : x + 1, :], 0.0)
        rest = jnp.zeros((nz - 8, ny), jnp.float32)
        z0, z1 = jnp.concatenate([z0, rest], 0), jnp.concatenate([z1, rest], 0)
        add0, add1, add2 = y2 - z1, z0, -y0
        if x == 0:
            add1 = add1 - hx_in[1]
            add2 = add2 + hx_in[0]
        en[0, x] = en[0, x] + coef * add0
        en[1, x] = en[1, x] + coef * add1
        en[2, x] = en[2, x] + coef * add2

    loads[3].wait()
    share = jnp.zeros((8, 128), jnp.float32)
    for p in range(NP):
        x_of = pidx_ref[p] - a * nx
        inside = (x_of >= 0) & (x_of < nx)
        at = jnp.clip(x_of, 0, nx - 1)
        both = modes[p, 0] * en[1, at] + modes[p, 1] * en[2, at]
        total = functools.reduce(jnp.add, tiles(both))
        total = jnp.sum(jnp.sum(total, axis=0, keepdims=True), axis=1, keepdims=True)
        total = jnp.where(inside, total, 0.0)
        share = jnp.where(lane8 == p, total, share)

    mine[...] = share[0:1]
    if n_gz > 1:
        pl.semaphore_wait(known_sems.at[1], n_gz - 1)

    def send_row(k, _):
        remote(mine, rows.at[k - 1], all_send, all_recv, lax.rem(me + k, n)).start()
        return 0

    lax.fori_loop(1, n, send_row, 0, unroll=n <= UNROLL)
    for i in (0, 2):
        pl.when(down[i][0])(e_copies[i].start)
    ey_out[...] = pack_lane([en[comp, x] for comp in (0, 2) for x in range(nx)], 0, lane8)
    pl.when(down[1][0])(e_copies[1].start)

    for i in range(3):
        pl.when(up[i][0])(h_copies[i].wait_send)
    loads[4].wait()

    def high(plane, axis):
        last = (row == nz - 1) if axis == 0 else (lane == ny - 1)
        return jnp.where(last, 0.0, pltpu.roll(plane, plane.shape[axis] - 1, axis)) - plane

    for x in range(nx):
        e0, e1, e2 = en[0, x], en[1, x], en[2, x]
        d1 = en[1, x + 1] - e1 if x < nx - 1 else -e1
        d2 = en[2, x + 1] - e2 if x < nx - 1 else -e2
        coef = hc[x]
        hn[0, x] = hn[0, x] + coef * (high(e2, 1) - high(e1, 0))
        hn[1, x] = hn[1, x] + coef * (high(e0, 0) - d2)
        hn[2, x] = hn[2, x] + coef * (d1 - high(e0, 1))

    loads[5].wait()
    loads[6].wait()
    for x in range(nx):
        product = weight * (ef[0, x] * en[0, x] + ef[1, x] * en[1, x] + ef[2, x] * en[2, x])
        for f in range(NF):
            dn[f, x] = dn[f, x] + cosines[f : f + 1] * product
            dn[NF + f, x] = dn[NF + f, x] + sines[f : f + 1] * product

    for i, landing in enumerate((ex_in, ey_in, ez_in)):
        pl.when(up[i][0])(e_copies[i].wait_recv)

        @pl.when(jnp.logical_not(up[i][0]))
        def _(landing=landing):
            landing[...] = jnp.zeros_like(landing)

    packed = ey_in[...]
    for x in range(nx):
        coef = hc[x]
        y0 = unpack_lane(packed, x * zt, zt, ny - 1, lane == ny - 1)
        y2 = unpack_lane(packed, (nx + x) * zt, zt, ny - 1, lane == ny - 1)
        z0 = jnp.where(sub8 == 7, ez_in[0, x : x + 1, :], 0.0)
        z1 = jnp.where(sub8 == 7, ez_in[1, x : x + 1, :], 0.0)
        rest = jnp.zeros((nz - 8, ny), jnp.float32)
        z0, z1 = jnp.concatenate([rest, z0], 0), jnp.concatenate([rest, z1], 0)
        add0, add1, add2 = y2 - z1, z0, -y0
        if x == nx - 1:
            add1 = add1 - ex_in[1]
            add2 = add2 + ex_in[0]
        hn[0, x] = hn[0, x] + coef * add0
        hn[1, x] = hn[1, x] + coef * add1
        hn[2, x] = hn[2, x] + coef * add2
    for i in range(3):
        pl.when(down[i][0])(e_copies[i].wait_send)

    remote(rows, rows, all_send, all_recv, me).wait()
    intersection = jnp.sum(rows[...], axis=0) + mine[...]
    lane1 = lax.broadcasted_iota(jnp.int32, (1, 128), 1)
    owned = jnp.zeros((1, 128), jnp.float32)
    for p in range(NP):
        owned = jnp.where(lane1 == p, (powner_ref[p] == me).astype(jnp.float32), owned)
    total = jnp.sum(owned * intersection, axis=1, keepdims=True)
    mon_out[...] = mon_ref[...] + total * phase_lanes[0:1, : 2 * NF]


def write_out(en, hn, dn, mon, en_out, hn_out, dn_out, mon_out, sems):
    parts = 4
    size = dn.shape[0] // parts
    pairs = [(dn.at[pl.ds(i * size, size)], dn_out.at[pl.ds(i * size, size)]) for i in range(parts)]
    pairs += [(en, en_out), (hn, hn_out), (mon, mon_out)]
    copies = [pltpu.make_async_copy(src, dst, sems.at[i]) for i, (src, dst) in enumerate(pairs)]
    for copy in copies:
        copy.start()
    for copy in copies:
        copy.wait()


def body(sizes, e_field, h_field, e_forward, e_coeff, h_coeff, dft_acc, design_mask,
         omega_t, port_index, port_owner, port_modes, monitor_acc):
    nx, nz, ny = e_coeff.shape
    n = sizes[0] * sizes[1] * sizes[2]
    f32 = jnp.float32
    hbm = pl.BlockSpec(memory_space=pltpu.HBM)
    vmem = pl.BlockSpec(memory_space=pltpu.VMEM)
    far = lambda x: pltpu.with_memory_space_constraint(x, pltpu.HBM)
    held = pl.pallas_call(
        functools.partial(step, sizes),
        out_shape=[
            pltpu.VMEM(e_field.shape, f32),
            pltpu.VMEM(h_field.shape, f32),
            pltpu.VMEM(dft_acc.shape, f32),
            pltpu.VMEM(monitor_acc.shape, f32),
        ],
        in_specs=[hbm] * 12,
        out_specs=[vmem] * 4,
        scratch_shapes=[
            pltpu.VMEM(e_forward.shape, f32),
            pltpu.VMEM(e_coeff.shape, f32),
            pltpu.VMEM(h_coeff.shape, f32),
            pltpu.VMEM(port_modes.shape, f32),
            pltpu.SMEM(design_mask.shape, jnp.int32),
            pltpu.SMEM(omega_t.shape, f32),
            pltpu.SMEM(port_index.shape, jnp.int32),
            pltpu.SMEM(port_owner.shape, jnp.int32),
            pltpu.VMEM(monitor_acc.shape, f32),
            pltpu.VMEM((2, nz, ny), f32),
            pltpu.VMEM((8, 128), f32),
            pltpu.VMEM((2, nx, ny), f32),
            pltpu.VMEM((2, nz, ny), f32),
            pltpu.VMEM((8, 128), f32),
            pltpu.VMEM((2, nx, ny), f32),
            pltpu.VMEM((8, 128), f32),
            pltpu.VMEM((8, 128), f32),
            pltpu.VMEM((1, 128), f32),
            pltpu.VMEM((n - 1, 1, 128), f32),
            pltpu.SemaphoreType.DMA((12,)),
            pltpu.SemaphoreType.DMA((3,)),
            pltpu.SemaphoreType.DMA((3,)),
            pltpu.SemaphoreType.DMA((3,)),
            pltpu.SemaphoreType.DMA((3,)),
            pltpu.SemaphoreType.DMA,
            pltpu.SemaphoreType.DMA,
            pltpu.SemaphoreType.REGULAR((2,)),
        ],
        compiler_params=pltpu.CompilerParams(
            collective_id=0, has_side_effects=True, vmem_limit_bytes=24 * 2**20
        ),
        name="yee_step",
    )(*map(far, (e_field, h_field, e_forward, e_coeff, h_coeff, dft_acc, port_modes,
      design_mask, omega_t, port_index, port_owner, monitor_acc)))
    shape = lambda x: jax.ShapeDtypeStruct(x.shape, f32)
    return pl.pallas_call(
        write_out,
        out_shape=[shape(x) for x in (e_field, h_field, dft_acc, monitor_acc)],
        in_specs=[vmem] * 4,
        out_specs=[hbm] * 4,
        scratch_shapes=[pltpu.SemaphoreType.DMA((7,))],
        name="write_out",
    )(*[pltpu.with_memory_space_constraint(x, pltpu.VMEM) for x in held])


def solution(mesh):
    grid = P(None, "gx", "gz", "gy")
    brick = P("gx", "gz", "gy")
    own = P(("gx", "gy", "gz"), None)
    sizes = tuple(mesh.shape[axis] for axis in ("gx", "gy", "gz"))
    in_specs = (grid, grid, grid, brick, brick, grid, brick, P(), P(), P(),
                P(None, None, "gz", "gy"), own)
    return jax.shard_map(
        functools.partial(body, sizes), mesh=mesh, in_specs=in_specs,
        out_specs=(grid, grid, grid, own), check_vma=False,
    )
```
